256 devices in a mesh: pairs: 64 (over z_hi, y, x), dates: 4 (over z_lo, core).
Axes of the slice: x: 4, y: 4, z: 8 (z_hi: 4, z_lo: 2; z = z_hi * 2 + z_lo), core: 2. Of those that a mesh axis runs over, the one named last changes fastest.
Arguments:
- returns: bfloat16 [4096, 32768], P('dates', 'pairs'), may hold values from -16 to 16
- plan: int32 [3, 64], P(None, 'pairs'), may hold values from 0 to 1
Outputs:
- rotated_panel: bfloat16 [4096, 32768], P('dates', 'pairs')
- disorder: float32 [3], replicated
The draws below stay inside these ranges and needn't reach their ends.
All inputs are finite; a program needn't handle non-finite values.
Results may differ from the reference program's by a relative error of at most 0.0067.
Values may be sent and summed in bfloat16 or wider, within the bound.
A program may use at most 64 MiB of HBM per device.

```python
import jax
import jax.numpy as jnp
from jax import lax

B = 256
ROUNDS = 3
NS_STEPS = 3
ROWS = 4096
SERIES = 32768
N_PAIRS = 64


def draw_returns(key, part):
    key_factor, key_loading, key_strength, key_noise_scale, key_noise = jax.random.split(jax.random.fold_in(key, 17), 5)
    factors = jax.random.normal(key_factor, (ROWS, 8), jnp.float32)
    loadings = jax.random.normal(key_loading, (SERIES, 8), jnp.float32)
    position = jnp.arange(SERIES, dtype=jnp.float32) / SERIES
    strength = (0.3 + 1.2 * position) * jax.random.uniform(key_strength, (SERIES,), jnp.float32, 0.5, 1.5)
    noise_scale = jnp.exp(jax.random.uniform(key_noise_scale, (SERIES,), jnp.float32, -0.7, 0.7))
    noise = jax.random.normal(key_noise, (ROWS, SERIES), jnp.float32)
    common = jnp.dot(factors, loadings.T) * (strength / jnp.sqrt(8.0))[None, :]
    values = common + noise * noise_scale[None, :]
    return jnp.clip(values, -16.0, 16.0).astype(jnp.bfloat16)


def touch_ends(values, rng, smallest, largest):
    place = [jax.random.randint(jax.random.fold_in(rng, axis), (), 0, length) for axis, length in enumerate(values.shape)]
    widest = values.shape.index(max(values.shape))
    neighbour = place[:widest] + [(place[widest] + 1) % values.shape[widest]] + place[widest + 1:]
    return values.at[tuple(place)].set(smallest).at[tuple(neighbour)].set(largest)


def setup_inputs(seed: int = 0) -> dict:
    arg_keys = jax.random.split(jax.random.key(seed), 3)
    returns = draw_returns(jax.random.fold_in(arg_keys[2], 71), 0)
    plan = touch_ends(jax.random.randint(arg_keys[1], (ROUNDS, N_PAIRS), 0, 2), jax.random.fold_in(arg_keys[1], 1), 0, 1).astype(jnp.int32)
    return {"returns": returns, "plan": plan}


damping_base = 0.5
epsilon = 1e-06

def reference(returns, plan):
    highest = lax.Precision.HIGHEST
    blocks = returns.reshape(ROWS, N_PAIRS, 2, B).transpose(1, 2, 0, 3)
    identity = jnp.eye(2 * B, dtype=jnp.float32)
    history = []
    for step_index in range(ROUNDS):
        joined = jnp.concatenate([blocks[:, 0], blocks[:, 1]], axis=2).astype(jnp.float32)
        gram = jnp.einsum('pmi,pmj->pij', joined, joined, precision=highest)
        diag_sum = jnp.diagonal(gram, axis1=1, axis2=2) + epsilon
        col_scale = jnp.sqrt(diag_sum)
        cross_block = gram[:, :B, B:] / (col_scale[:, :B, None] * col_scale[:, None, B:])
        coupling = lax.optimization_barrier(jnp.sum(cross_block * cross_block, axis=(1, 2)))
        overall = jnp.sum(coupling / (B * B))
        history.append(overall)
        damping = damping_base / jnp.sqrt(1.0 + B * B * overall / N_PAIRS)
        zeros_block = jnp.zeros_like(cross_block)
        skew_part = jnp.concatenate([jnp.concatenate([zeros_block, -cross_block], axis=2), jnp.concatenate([jnp.transpose(cross_block, (0, 2, 1)), zeros_block], axis=2)], axis=1)
        factor = (identity + damping * skew_part) / jnp.sqrt(1.0 + 2.0 * damping * damping * coupling)[:, None, None]
        for inner_step in range(NS_STEPS):
            squared = jnp.einsum('pab,pac->pbc', factor, factor, precision=highest)
            factor = 1.5 * factor - 0.5 * jnp.einsum('pab,pbc->pac', factor, squared, precision=highest)
        rotation = lax.optimization_barrier(factor.astype(jnp.bfloat16)).astype(jnp.float32)
        rotated = jnp.einsum('pmi,pij->pmj', joined, rotation, precision=highest).astype(jnp.bfloat16)
        front_half = rotated[:, :, :B]
        back_half = rotated[:, :, B:]
        chosen = plan[step_index][:, None, None]
        outgoing = jnp.where(chosen == 0, front_half, back_half)
        incoming = jnp.roll(outgoing, 1, axis=0)
        slot_zero = jnp.where(chosen == 0, incoming, front_half)
        slot_one = jnp.where(chosen == 1, incoming, back_half)
        blocks = jnp.stack([slot_zero, slot_one], axis=1)
    rotated_panel = blocks.transpose(2, 0, 1, 3).reshape(ROWS, SERIES)
    return (rotated_panel, jnp.stack(history))
```

```python
import functools

import jax
import jax.numpy as jnp
from jax import lax
from jax.experimental import pallas as pl
from jax.experimental.pallas import tpu as pltpu
from jax.sharding import PartitionSpec as P

ROUNDS = 3
damping_base = 0.5
epsilon = 1e-06
MESH = pl.DeviceIdType.MESH
F32 = jnp.float32
BF16 = jnp.bfloat16
PIECES = 4
RELAYED = (2, 3)


def mm(a, b):
    return jnp.dot(a.astype(BF16), b.astype(BF16), preferred_element_type=F32)


def mm_tn(a, b):
    return lax.dot_general(a, b, (((0,), (0,)), ((), ())), preferred_element_type=F32)


def send(src, dst, send_sem, recv_sem, device):
    return pltpu.make_async_remote_copy(
        src_ref=src, dst_ref=dst, send_sem=send_sem, recv_sem=recv_sem, device_id=device, device_id_type=MESH
    )


def steps_between(k, n_pairs, row):
    x, y, z = k % row, (k // row) % row, k // (row * row)
    depth = n_pairs // (row * row)
    return min(x, row - x) + min(y, row - y) + 2 * min(z, depth - z)


class Side:
    def __init__(self, m):
        self.m = m
        self.m2 = mm(m, m)
        self.m3 = mm(self.m2, m)

    def finish(self, n, t):
        w = 1.5 - 0.5 * n
        tau = n * w * w
        e = t * (w * w - n * w) * self.m + t * t * (0.25 * n - w) * self.m2 + (0.25 * t * t * t) * self.m3
        w1 = 1.5 - 0.5 * tau
        e2 = mm(e, e)
        y = t * self.m
        self.gb = (-0.5 * w) * e - (0.5 * w1) * y + 0.25 * mm(y, e)
        self.hb = w * w1
        e3 = mm(e, e2)
        self.f = -0.5 * ((w1 * w1 - tau * w1) * e + (0.25 * tau - w1) * e2 + 0.25 * e3)
        self.w2 = 1.5 - 0.5 * tau * w1 * w1
        self.h = self.hb * self.w2
        self.hn = self.hb * self.f + self.w2 * self.gb + mm(self.gb, self.f)

    def right_of(self, d):
        r = self.hb * d + mm(d, self.gb)
        return self.w2 * r + mm(r, self.f)


def kernel(n_pairs, n_dates, x_ref, plan_ref, inc_out, stay_out, dis_ref,
           inc_buf, mov_buf, relay_buf, stay_buf, pan, gram_buf, share, shares,
           ring_send, ring_recv, relay_send, relay_recv, fwd_send, gram_send, gram_recv, share_send, share_recv):
    rows, b2 = x_ref.shape
    b = b2 // 2
    half = b // 2
    height = rows // PIECES
    plane = n_pairs // 4
    p, d = lax.axis_index("pairs"), lax.axis_index("dates")
    following = lax.rem(p + 1, n_pairs)

    barrier = pltpu.get_barrier_semaphore()
    for k in range(1, n_pairs):
        pl.semaphore_signal(barrier, inc=1, device_id=(lax.rem(p + k, n_pairs), d), device_id_type=MESH)
    for k in range(1, n_dates):
        pl.semaphore_signal(barrier, inc=1, device_id=(p, lax.rem(d + k, n_dates)), device_id_type=MESH)

    is_corner = lax.rem(p, plane) == plane - 1
    is_relay = lax.rem(p, plane) == 0
    relay_at = lax.rem(p - (plane - 1) + n_pairs, n_pairs)
    relay_to = lax.rem(p + plane, n_pairs)

    eye_half = lax.broadcasted_iota(jnp.int32, (half, half), 0) == lax.broadcasted_iota(jnp.int32, (half, half), 1)
    eye = (lax.broadcasted_iota(jnp.int32, (b, b), 0) == lax.broadcasted_iota(jnp.int32, (b, b), 1)).astype(F32)
    extra_row = lax.broadcasted_iota(jnp.int32, (16, b), 0)
    order = sorted(range(1, n_pairs), key=lambda k: -steps_between(k, n_pairs, 4))
    pieces = [(c, i) for c in range(2) for i in range(PIECES)]
    relayed = [(c, i) for c in range(2) for i in RELAYED]

    def split(v):
        hi = v.astype(BF16).astype(F32)
        return hi, v - hi

    previous_slot = None
    for r in range(ROUNDS):
        slot = plan_ref[r, 0]
        if r == 0:
            moves_inc = slot == 0
            inc = [x_ref.at[:, pl.ds(half * c, half)] for c in range(2)]
            stay = x_ref.at[:, pl.ds(b, b)]
        else:
            moves_inc = slot == previous_slot
            inc = [inc_buf.at[r - 1, c] for c in range(2)]
            stay = stay_buf.at[r - 1]
        previous_slot = slot
        sign = jnp.where(slot == 0, 1.0, -1.0).astype(F32)

        stay_f32 = stay[...].astype(F32)
        stay_sq = jnp.sum(stay_f32 * stay_f32, axis=0, keepdims=True)
        stay_hi, stay_lo = split(stay_sq)
        gram_copies = []
        for c in range(2):
            if r > 0:
                for i in range(PIECES):
                    incoming[c, i].wait_recv()
            inc_f32 = inc[c][...].astype(F32)
            inc_hi, inc_lo = split(jnp.sum(inc_f32 * inc_f32, axis=0, keepdims=True))
            mine = gram_buf.at[r, c, d]
            mine[0:half, :] = mm_tn(inc[c][...], stay[...]).astype(BF16)
            extra = jnp.where(extra_row == 0, jnp.concatenate([inc_hi, inc_lo], axis=1), 0.0)
            extra = jnp.where(extra_row == 1, stay_hi, extra)
            extra = jnp.where(extra_row == 2, stay_lo, extra)
            mine[half:half + 16, :] = extra.astype(BF16)
            if r == 0 and c == 0:
                pl.semaphore_wait(barrier, n_pairs - 1 + n_dates - 1)
            for k in range(1, n_dates):
                copy = send(mine, mine, gram_send.at[r, c, k - 1], gram_recv.at[r, c, k - 1], (p, lax.rem(d + k, n_dates)))
                copy.start()
                gram_copies.append(copy)
            if r > 0 and c == 0:
                forward(1)
        cross = []
        for c in range(2):
            for k in range(n_dates - 1):
                gram_copies[c * (n_dates - 1) + k].wait_recv()
            total = gram_buf[r, c, 0].astype(F32)
            for k in range(1, n_dates):
                total = total + gram_buf[r, c, k].astype(F32)
            inc_scale = lax.rsqrt(total[half:half + 1, :half] + total[half:half + 1, half:] + epsilon)
            stay_scale = lax.rsqrt(total[half + 1:half + 2] + total[half + 2:half + 3] + epsilon)
            inc_scale = jnp.sum(jnp.where(eye_half, inc_scale, 0.0), axis=1, keepdims=True)
            cross.append(total[0:half] * inc_scale * stay_scale)
        cross = jnp.concatenate(cross, axis=0)
        coupling = jnp.sum(jnp.sum(cross * cross, axis=0, keepdims=True), axis=1, keepdims=True)

        mine = jnp.broadcast_to(coupling * (1.0 / (b * b)), (8, 128))
        share[r] = mine
        shares[r, pl.ds(p, 1), :] = mine[0:1]
        share_copies = []
        for k in order:
            copy = send(share.at[r, pl.ds(0, 1)], shares.at[r, pl.ds(p, 1)], share_send.at[r], share_recv.at[r],
                        (lax.rem(p + k, n_pairs), d))
            copy.start()
            share_copies.append(copy)

        cross_t = cross.T
        d_mov = lax.select(moves_inc, cross, cross_t)
        d_mov_t = lax.select(moves_inc, cross_t, cross)
        mov_side = Side(mm(d_mov, d_mov_t))
        stay_side = Side(mm(d_mov_t, d_mov))
        for c in range(2):
            one, two = inc[c][...], stay[:, half * c:half * (c + 1)]
            pan[:, half * c:half * (c + 1)] = lax.select(moves_inc, one, two)
            pan[:, b + half * c:b + half * (c + 1)] = lax.select(moves_inc, two, one)

        everyone = send(shares.at[r, pl.ds(0, n_pairs - 1)], shares.at[r, pl.ds(0, n_pairs - 1)], share_send.at[r],
                        share_recv.at[r], (following, d))
        everyone.wait_recv()
        overall = jnp.sum(shares[r], axis=0, keepdims=True)
        dis_ref[r:r + 1, :] = overall
        overall = overall[:, 0:1]
        damping = damping_base / jnp.sqrt(1.0 + float(b * b) * overall / n_pairs)
        n = 1.0 / (1.0 + 2.0 * damping * damping * coupling)
        t = n * damping * damping
        a = jnp.sqrt(n)
        ad = a * damping * sign

        mov_side.finish(n, t)
        top = a * mov_side.h * eye + a * mov_side.hn
        bottom = ad * mov_side.right_of(d_mov_t)
        rotation = jnp.concatenate([top, bottom], axis=0).astype(BF16)

        landing = inc_out if r == ROUNDS - 1 else inc_buf.at[r]
        incoming, by_relay, forwards = {}, {}, {}
        for q, (c, i) in enumerate(pieces):
            place = pl.ds(height * i, height)
            incoming[c, i] = send(mov_buf.at[r, c, place], landing.at[c, place], ring_send.at[r, q], ring_recv.at[r, q], (following, d))
        for q, (c, i) in enumerate(relayed):
            place = pl.ds(height * i, height)
            way = relay_buf.at[r, q]
            by_relay[c, i] = send(mov_buf.at[r, c, place], way, relay_send.at[r, q], relay_recv.at[r, q], (relay_at, d))
            forwards[c, i] = send(way, landing.at[c, place], fwd_send.at[r, q], ring_recv.at[r, c * PIECES + i], (relay_to, d))

        def pass_on(c, i, incoming=incoming, by_relay=by_relay):
            if i in RELAYED:
                @pl.when(is_corner)
                def _():
                    by_relay[c, i].start()

                @pl.when(jnp.logical_not(is_corner))
                def _():
                    incoming[c, i].start()
            else:
                incoming[c, i].start()

        def forward(c, by_relay=by_relay, forwards=forwards):
            @pl.when(is_relay)
            def _():
                for i in RELAYED:
                    by_relay[c, i].wait_recv()
                    forwards[c, i].start()

        for i in range(PIECES):
            place = pl.ds(height * i, height)
            part = jnp.dot(pan[place, :], rotation, preferred_element_type=F32).astype(BF16)
            mov_buf[r, 0, place, :] = part[:, :half]
            mov_buf[r, 1, place, :] = part[:, half:]
            pass_on(0, i)
        for i in range(PIECES):
            pass_on(1, i)

        stay_side.finish(n, t)
        top = (-ad) * stay_side.right_of(d_mov)
        bottom = a * stay_side.h * eye + a * stay_side.hn
        rotation = jnp.concatenate([top, bottom], axis=0).astype(BF16)
        target = stay_out if r == ROUNDS - 1 else stay_buf.at[r]
        target[...] = jnp.dot(pan[...], rotation, preferred_element_type=F32).astype(BF16)
        forward(0)

        for copy in gram_copies:
            copy.wait_send()
        everyone.wait_send()
        if r == ROUNDS - 1:
            forward(1)
            for c, i in pieces:
                incoming[c, i].wait_recv()
        def finish(incoming=incoming, by_relay=by_relay, forwards=forwards):
            for c, i in pieces:
                if i in RELAYED:
                    @pl.when(is_corner)
                    def _():
                        by_relay[c, i].wait_send()

                    @pl.when(jnp.logical_not(is_corner))
                    def _():
                        incoming[c, i].wait_send()
                else:
                    incoming[c, i].wait_send()

            @pl.when(is_relay)
            def _():
                for k in relayed:
                    forwards[k].wait_send()
        finishes = [finish] if r == 0 else finishes + [finish]
    for finish in finishes:
        finish()


def local(n_pairs, n_dates, returns, plan):
    rows, b2 = returns.shape
    b = b2 // 2
    half = b // 2
    height = rows // PIECES
    dma = pltpu.SemaphoreType.DMA
    vmem = pl.BlockSpec(memory_space=pltpu.VMEM)
    moved, stayed, disorder = pl.pallas_call(
        functools.partial(kernel, n_pairs, n_dates),
        out_shape=(
            jax.ShapeDtypeStruct((2, rows, half), BF16),
            jax.ShapeDtypeStruct((rows, b), BF16),
            jax.ShapeDtypeStruct((8, 128), F32),
        ),
        in_specs=[vmem, pl.BlockSpec(memory_space=pltpu.SMEM)],
        out_specs=(vmem, vmem, vmem),
        scratch_shapes=[
            pltpu.VMEM((ROUNDS - 1, 2, rows, half), BF16),
            pltpu.VMEM((ROUNDS, 2, rows, half), BF16),
            pltpu.VMEM((ROUNDS, 2 * len(RELAYED), height, half), BF16),
            pltpu.VMEM((ROUNDS - 1, rows, b), BF16),
            pltpu.VMEM((rows, b2), BF16),
            pltpu.VMEM((ROUNDS, 2, n_dates, half + 16, b), BF16),
            pltpu.VMEM((ROUNDS, 8, 128), F32),
            pltpu.VMEM((ROUNDS, n_pairs, 128), F32),
            dma((ROUNDS, 2 * PIECES)),
            dma((ROUNDS, 2 * PIECES)),
            dma((ROUNDS, 2 * len(RELAYED))),
            dma((ROUNDS, 2 * len(RELAYED))),
            dma((ROUNDS, 2 * len(RELAYED))),
            dma((ROUNDS, 2, n_dates - 1)),
            dma((ROUNDS, 2, n_dates - 1)),
            dma((ROUNDS,)),
            dma((ROUNDS,)),
        ],
        compiler_params=pltpu.CompilerParams(collective_id=0, has_side_effects=True, vmem_limit_bytes=48 << 20),
        name="jacobi_rounds",
    )(returns, plan)
    front = jnp.concatenate([moved[0], moved[1], stayed], axis=1)
    back = jnp.concatenate([stayed, moved[0], moved[1]], axis=1)
    return jnp.where(plan[ROUNDS - 1, 0] == 0, front, back), disorder[:ROUNDS, 0]


def solution(mesh):
    return jax.shard_map(
        functools.partial(local, mesh.shape["pairs"], mesh.shape["dates"]),
        mesh=mesh,
        in_specs=(P("dates", "pairs"), P(None, "pairs")),
        out_specs=(P("dates", "pairs"), P()),
        check_vma=False,
    )
```

```python
import functools

import jax
import jax.numpy as jnp
from jax import lax
from jax.experimental import pallas as pl
from jax.experimental.pallas import tpu as pltpu
from jax.sharding import PartitionSpec as P

ROUNDS = 3
damping_base = 0.5
epsilon = 1e-06
MESH = pl.DeviceIdType.MESH
F32 = jnp.float32
BF16 = jnp.bfloat16
PIECES = 4
WAYS = ((0, 1, 2, None), (0, 1, 2, None))


def mm(a, b):
    return jnp.dot(a.astype(BF16), b.astype(BF16), preferred_element_type=F32)


def mm_tn(a, b):
    return lax.dot_general(a, b, (((0,), (0,)), ((), ())), preferred_element_type=F32)


def send(src, dst, send_sem, recv_sem, device):
    return pltpu.make_async_remote_copy(
        src_ref=src, dst_ref=dst, send_sem=send_sem, recv_sem=recv_sem, device_id=device, device_id_type=MESH
    )


def steps_between(k, n_pairs, row):
    x, y, z = k % row, (k // row) % row, k // (row * row)
    depth = n_pairs // (row * row)
    return min(x, row - x) + min(y, row - y) + 2 * min(z, depth - z)


class Side:
    def __init__(self, m):
        self.m = m
        self.m2 = mm(m, m)
        self.m3 = mm(self.m2, m)

    def finish(self, n, t):
        w = 1.5 - 0.5 * n
        tau = n * w * w
        e = t * (w * w - n * w) * self.m + t * t * (0.25 * n - w) * self.m2 + (0.25 * t * t * t) * self.m3
        w1 = 1.5 - 0.5 * tau
        e2 = mm(e, e)
        y = t * self.m
        self.gb = (-0.5 * w) * e - (0.5 * w1) * y + 0.25 * mm(y, e)
        self.hb = w * w1
        e3 = mm(e, e2)
        self.f = -0.5 * ((w1 * w1 - tau * w1) * e + (0.25 * tau - w1) * e2 + 0.25 * e3)
        self.w2 = 1.5 - 0.5 * tau * w1 * w1
        self.h = self.hb * self.w2
        self.hn = self.hb * self.f + self.w2 * self.gb + mm(self.gb, self.f)

    def right_of(self, d):
        r = self.hb * d + mm(d, self.gb)
        return self.w2 * r + mm(r, self.f)


def kernel(n_pairs, n_dates, panel_ref, plan_ref, out_ref, dis_ref,
           x_ref, x_sem, inc_buf, mov_buf, relay_buf, stay_buf, pan, gram_buf, share, shares,
           ring_send, ring_recv, relay_send, relay_recv, fwd_send, gram_send, gram_recv, share_send, share_recv):
    rows, b2 = panel_ref.shape
    b = b2 // 2
    half = b // 2
    height = rows // PIECES
    plane = n_pairs // 4
    p, d = lax.axis_index("pairs"), lax.axis_index("dates")
    fetch = [pltpu.make_async_copy(panel_ref.at[:, pl.ds(b * k, b)], x_ref.at[:, pl.ds(b * k, b)], x_sem.at[k]) for k in range(2)]
    for copy in reversed(fetch):
        copy.start()
    following = lax.rem(p + 1, n_pairs)

    barrier = pltpu.get_barrier_semaphore()
    for k in range(1, n_pairs):
        pl.semaphore_signal(barrier, inc=1, device_id=(lax.rem(p + k, n_pairs), d), device_id_type=MESH)
    for k in range(1, n_dates):
        pl.semaphore_signal(barrier, inc=1, device_id=(p, lax.rem(d + k, n_dates)), device_id_type=MESH)

    back = (plane - 1, 3, plane - 4)
    is_corner = lax.rem(p, plane) == plane - 1
    is_relay = [lax.rem(p + k, plane) == plane - 1 for k in back]
    relay_at = [lax.rem(p - k + n_pairs, n_pairs) for k in back]
    relay_to = [lax.rem(p + k + 1, n_pairs) for k in back]

    eye_half = lax.broadcasted_iota(jnp.int32, (half, half), 0) == lax.broadcasted_iota(jnp.int32, (half, half), 1)
    eye = (lax.broadcasted_iota(jnp.int32, (b, b), 0) == lax.broadcasted_iota(jnp.int32, (b, b), 1)).astype(F32)
    extra_row = lax.broadcasted_iota(jnp.int32, (16, b), 0)
    order = sorted(range(1, n_pairs), key=lambda k: -steps_between(k, n_pairs, 4))
    pieces = [(c, i) for c in range(2) for i in range(PIECES)]

    def split(v):
        hi = v.astype(BF16).astype(F32)
        return hi, v - hi

    previous_slot = None
    for r in range(ROUNDS):
        slot = plan_ref[r]
        if r == 0:
            fetch[1].wait()
            moves_inc = slot == 0
            inc = [x_ref.at[:, pl.ds(half * c, half)] for c in range(2)]
            stay = x_ref.at[:, pl.ds(b, b)]
        else:
            moves_inc = slot == previous_slot
            inc = [inc_buf.at[r - 1, c] for c in range(2)]
            stay = stay_buf.at[r - 1]
        previous_slot = slot
        sign = jnp.where(slot == 0, 1.0, -1.0).astype(F32)

        stay_f32 = stay[...].astype(F32)
        stay_sq = jnp.sum(stay_f32 * stay_f32, axis=0, keepdims=True)
        stay_hi, stay_lo = split(stay_sq)
        gram_copies = []
        for c in range(2):
            if r > 0:
                for i in range(PIECES):
                    incoming[c, i].wait_recv()
            if r == 0 and c == 0:
                fetch[0].wait()
            inc_f32 = inc[c][...].astype(F32)
            inc_hi, inc_lo = split(jnp.sum(inc_f32 * inc_f32, axis=0, keepdims=True))
            mine = gram_buf.at[r, c, d]
            mine[0:half, :] = mm_tn(inc[c][...], stay[...]).astype(BF16)
            extra = jnp.where(extra_row == 0, jnp.concatenate([inc_hi, inc_lo], axis=1), 0.0)
            extra = jnp.where(extra_row == 1, stay_hi, extra)
            extra = jnp.where(extra_row == 2, stay_lo, extra)
            mine[half:half + 16, :] = extra.astype(BF16)
            if r == 0 and c == 0:
                pl.semaphore_wait(barrier, n_pairs - 1 + n_dates - 1)
            for k in range(1, n_dates):
                copy = send(mine, mine, gram_send.at[r, c, k - 1], gram_recv.at[r, c, k - 1], (p, lax.rem(d + k, n_dates)))
                copy.start()
                gram_copies.append(copy)
        cross = []
        for c in range(2):
            for k in range(n_dates - 1):
                gram_copies[c * (n_dates - 1) + k].wait_recv()
            total = gram_buf[r, c, 0].astype(F32)
            for k in range(1, n_dates):
                total = total + gram_buf[r, c, k].astype(F32)
            inc_scale = lax.rsqrt(total[half:half + 1, :half] + total[half:half + 1, half:] + epsilon)
            stay_scale = lax.rsqrt(total[half + 1:half + 2] + total[half + 2:half + 3] + epsilon)
            inc_scale = jnp.sum(jnp.where(eye_half, inc_scale, 0.0), axis=1, keepdims=True)
            cross.append(total[0:half] * inc_scale * stay_scale)
        cross = jnp.concatenate(cross, axis=0)
        coupling = jnp.sum(jnp.sum(cross * cross, axis=0, keepdims=True), axis=1, keepdims=True)

        mine = jnp.broadcast_to(coupling * (1.0 / (b * b)), (8, 128))
        share[r] = mine
        shares[r, pl.ds(p, 1), :] = mine[0:1]
        share_copies = []
        for k in order:
            copy = send(share.at[r, pl.ds(0, 1)], shares.at[r, pl.ds(p, 1)], share_send.at[r], share_recv.at[r],
                        (lax.rem(p + k, n_pairs), d))
            copy.start()
            share_copies.append(copy)

        cross_t = cross.T
        d_mov = lax.select(moves_inc, cross, cross_t)
        d_mov_t = lax.select(moves_inc, cross_t, cross)
        mov_side = Side(mm(d_mov, d_mov_t))
        stay_side = Side(mm(d_mov_t, d_mov))
        for c in range(2):
            one, two = inc[c][...], stay[:, half * c:half * (c + 1)]
            pan[:, half * c:half * (c + 1)] = lax.select(moves_inc, one, two)
            pan[:, b + half * c:b + half * (c + 1)] = lax.select(moves_inc, two, one)

        everyone = send(shares.at[r, pl.ds(0, n_pairs - 1)], shares.at[r, pl.ds(0, n_pairs - 1)], share_send.at[r],
                        share_recv.at[r], (following, d))
        everyone.wait_recv()
        overall = jnp.sum(shares[r], axis=0, keepdims=True)
        dis_ref[r:r + 1, :] = overall
        overall = overall[:, 0:1]
        damping = damping_base / jnp.sqrt(1.0 + float(b * b) * overall / n_pairs)
        n = 1.0 / (1.0 + 2.0 * damping * damping * coupling)
        t = n * damping * damping
        a = jnp.sqrt(n)
        ad = a * damping * sign

        mov_side.finish(n, t)
        top = a * mov_side.h * eye + a * mov_side.hn
        bottom = ad * mov_side.right_of(d_mov_t)
        rotation = jnp.concatenate([top, bottom], axis=0).astype(BF16)

        landing = inc_buf.at[r]
        incoming, by_relay, forwards = {}, {}, {}
        for q, (c, i) in enumerate(pieces):
            place = pl.ds(height * i, height)
            incoming[c, i] = send(mov_buf.at[r, c, place], landing.at[c, place], ring_send.at[r, q], ring_recv.at[r, q], (following, d))
            if WAYS[c][i] is None:
                continue
            way = relay_buf.at[r, q]
            by_relay[c, i] = send(mov_buf.at[r, c, place], way, relay_send.at[r, q], relay_recv.at[r, q], (relay_at[WAYS[c][i]], d))
            forwards[c, i] = send(way, landing.at[c, place], fwd_send.at[r, q], ring_recv.at[r, q], (relay_to[WAYS[c][i]], d))

        def pass_on(c, i, incoming=incoming, by_relay=by_relay):
            if WAYS[c][i] is None:
                incoming[c, i].start()
            else:
                @pl.when(is_corner)
                def _():
                    by_relay[c, i].start()

                @pl.when(jnp.logical_not(is_corner))
                def _():
                    incoming[c, i].start()

        def forward(by_relay=by_relay, forwards=forwards):
            for way, here in enumerate(is_relay):
                @pl.when(here)
                def _():
                    for c, i in pieces:
                        if WAYS[c][i] == way:
                            by_relay[c, i].wait_recv()
                            forwards[c, i].start()

        for i in range(PIECES):
            place = pl.ds(height * i, height)
            part = jnp.dot(pan[place, :], rotation, preferred_element_type=F32).astype(BF16)
            mov_buf[r, 0, place, :] = part[:, :half]
            mov_buf[r, 1, place, :] = part[:, half:]
            pass_on(0, i)
        for i in range(PIECES):
            pass_on(1, i)

        stay_side.finish(n, t)
        top = (-ad) * stay_side.right_of(d_mov)
        bottom = a * stay_side.h * eye + a * stay_side.hn
        rotation = jnp.concatenate([top, bottom], axis=0).astype(BF16)
        stay_buf[r] = jnp.dot(pan[...], rotation, preferred_element_type=F32).astype(BF16)
        forward()

        for copy in gram_copies:
            copy.wait_send()
        everyone.wait_send()
        if r == ROUNDS - 1:
            for c in range(2):
                for i in range(PIECES):
                    incoming[c, i].wait_recv()
                left, right = pl.ds(half * c, half), pl.ds(b + half * c, half)
                one, two = inc_buf[r, c], stay_buf[r, :, half * c:half * (c + 1)]
                out_ref[:, left] = lax.select(slot == 0, one, two)
                out_ref[:, right] = lax.select(slot == 0, two, one)
        def finish(incoming=incoming, by_relay=by_relay, forwards=forwards):
            for c, i in pieces:
                if WAYS[c][i] is None:
                    incoming[c, i].wait_send()
                else:
                    @pl.when(is_corner)
                    def _():
                        by_relay[c, i].wait_send()

                    @pl.when(jnp.logical_not(is_corner))
                    def _():
                        incoming[c, i].wait_send()

                    @pl.when(is_relay[WAYS[c][i]])
                    def _():
                        forwards[c, i].wait_send()
        finishes = [finish] if r == 0 else finishes + [finish]
    for finish in finishes:
        finish()


def local(n_pairs, n_dates, returns, plan):
    rows, b2 = returns.shape
    b = b2 // 2
    half = b // 2
    height = rows // PIECES
    dma = pltpu.SemaphoreType.DMA
    vmem = pl.BlockSpec(memory_space=pltpu.VMEM)
    rotated_panel, disorder = pl.pallas_call(
        functools.partial(kernel, n_pairs, n_dates),
        out_shape=(
            jax.ShapeDtypeStruct((rows, b2), BF16),
            jax.ShapeDtypeStruct((8, 128), F32),
        ),
        in_specs=[pl.BlockSpec(memory_space=pltpu.HBM), pl.BlockSpec(memory_space=pltpu.SMEM)],
        out_specs=(vmem, vmem),
        scratch_shapes=[
            pltpu.VMEM((rows, b2), BF16),
            dma((2,)),
            pltpu.VMEM((ROUNDS, 2, rows, half), BF16),
            pltpu.VMEM((ROUNDS, 2, rows, half), BF16),
            pltpu.VMEM((ROUNDS, 2 * PIECES, height, half), BF16),
            pltpu.VMEM((ROUNDS, rows, b), BF16),
            pltpu.VMEM((rows, b2), BF16),
            pltpu.VMEM((ROUNDS, 2, n_dates, half + 16, b), BF16),
            pltpu.VMEM((ROUNDS, 8, 128), F32),
            pltpu.VMEM((ROUNDS, n_pairs, 128), F32),
            dma((ROUNDS, 2 * PIECES)),
            dma((ROUNDS, 2 * PIECES)),
            dma((ROUNDS, 2 * PIECES)),
            dma((ROUNDS, 2 * PIECES)),
            dma((ROUNDS, 2 * PIECES)),
            dma((ROUNDS, 2, n_dates - 1)),
            dma((ROUNDS, 2, n_dates - 1)),
            dma((ROUNDS,)),
            dma((ROUNDS,)),
        ],
        compiler_params=pltpu.CompilerParams(collective_id=0, has_side_effects=True, vmem_limit_bytes=62 << 20),
        name="jacobi_rounds",
    )(returns, plan.reshape(ROUNDS))
    return rotated_panel, disorder[:ROUNDS, 0]


def solution(mesh):
    return jax.shard_map(
        functools.partial(local, mesh.shape["pairs"], mesh.shape["dates"]),
        mesh=mesh,
        in_specs=(P("dates", "pairs"), P(None, "pairs")),
        out_specs=(P("dates", "pairs"), P()),
        check_vma=False,
    )
```

```python
import functools

import jax
import jax.numpy as jnp
from jax import lax
from jax.experimental import pallas as pl
from jax.experimental.pallas import tpu as pltpu
from jax.sharding import PartitionSpec as P

ROUNDS = 3
damping_base = 0.5
epsilon = 1e-06
MESH = pl.DeviceIdType.MESH
F32 = jnp.float32
BF16 = jnp.bfloat16
PIECES = 8
STRAIGHT = None
WAYS = ((2,0,1,STRAIGHT,2,0,1,STRAIGHT),(2,0,1,STRAIGHT,2,STRAIGHT,STRAIGHT,STRAIGHT))


def mm(a, b):
    return jnp.dot(a.astype(BF16), b.astype(BF16), preferred_element_type=F32)


def mm_tn(a, b):
    return lax.dot_general(a, b, (((0,), (0,)), ((), ())), preferred_element_type=F32)


def send(src, dst, send_sem, recv_sem, device):
    return pltpu.make_async_remote_copy(
        src_ref=src, dst_ref=dst, send_sem=send_sem, recv_sem=recv_sem, device_id=device, device_id_type=MESH
    )


def chip_steps(n_pairs):
    depth = n_pairs // 16
    places = [(dz, dy, dx) for dz in range(depth) for dy in range(4) for dx in range(4) if (dz, dy, dx) != (0, 0, 0)]

    def chips(place):
        dz, dy, dx = place
        along_z = 2 * min(dz, depth - dz) - (2 * dz == depth)
        return along_z + min(dy, 4 - dy) + min(dx, 4 - dx)

    return sorted(places, key=chips, reverse=True)


class Side:
    def __init__(self, m):
        self.m = m
        self.m2 = mm(m, m)
        self.m3 = mm(self.m2, m)

    def finish(self, n, t):
        w = 1.5 - 0.5 * n
        tau = n * w * w
        e = t * (w * w - n * w) * self.m + t * t * (0.25 * n - w) * self.m2 + (0.25 * t * t * t) * self.m3
        w1 = 1.5 - 0.5 * tau
        e2 = mm(e, e)
        y = t * self.m
        self.gb = (-0.5 * w) * e - (0.5 * w1) * y + 0.25 * mm(y, e)
        self.hb = w * w1
        e3 = mm(e, e2)
        self.f = -0.5 * ((w1 * w1 - tau * w1) * e + (0.25 * tau - w1) * e2 + 0.25 * e3)
        self.w2 = 1.5 - 0.5 * tau * w1 * w1
        self.h = self.hb * self.w2
        self.hn = self.hb * self.f + self.w2 * self.gb + mm(self.gb, self.f)

    def right_of(self, d):
        r = self.hb * d + mm(d, self.gb)
        return self.w2 * r + mm(r, self.f)


def kernel(n_pairs, n_dates, panel_ref, plan_ref, out_ref, dis_ref,
           x_ref, x_sem, inc_buf, mov_buf, relay_buf, stay_buf, pan, gram_buf, share, shares,
           ring_send, ring_recv, relay_send, relay_recv, fwd_send, gram_send, gram_recv, share_send, share_recv):
    rows, b2 = panel_ref.shape
    b = b2 // 2
    half = b // 2
    height = rows // PIECES
    plane = n_pairs // 4
    p, d = lax.axis_index("pairs"), lax.axis_index("dates")
    fetch = [pltpu.make_async_copy(panel_ref.at[:, pl.ds(b * k, b)], x_ref.at[:, pl.ds(b * k, b)], x_sem.at[k]) for k in range(2)]
    for copy in reversed(fetch):
        copy.start()
    following = lax.rem(p + 1, n_pairs)

    depth = n_pairs // 16
    pz, py, px = p // 16, lax.rem(p // 4, 4), lax.rem(p, 4)
    partners = []
    for dz, dy, dx in chip_steps(n_pairs):
        pair = lax.rem(pz + dz, depth) * 16 + lax.rem(py + dy, 4) * 4 + lax.rem(px + dx, 4)
        partners.append((pair, lax.rem(d + n_dates // 2, n_dates) if 2 * dz == depth else d))

    barrier = pltpu.get_barrier_semaphore()
    for partner in partners:
        pl.semaphore_signal(barrier, inc=1, device_id=partner, device_id_type=MESH)
    for k in range(1, n_dates):
        pl.semaphore_signal(barrier, inc=1, device_id=(p, lax.rem(d + k, n_dates)), device_id_type=MESH)

    back = (plane - 1, 3, plane - 4)
    is_corner = lax.rem(p, plane) == plane - 1
    is_relay = [lax.rem(p + k, plane) == plane - 1 for k in back]
    relay_at = [lax.rem(p - k + n_pairs, n_pairs) for k in back]
    relay_to = [lax.rem(p + k + 1, n_pairs) for k in back]

    eye_half = lax.broadcasted_iota(jnp.int32, (half, half), 0) == lax.broadcasted_iota(jnp.int32, (half, half), 1)
    eye = (lax.broadcasted_iota(jnp.int32, (b, b), 0) == lax.broadcasted_iota(jnp.int32, (b, b), 1)).astype(F32)
    extra_row = lax.broadcasted_iota(jnp.int32, (16, b), 0)
    pieces = [(c, i) for c in range(2) for i in range(PIECES)]

    def split(v):
        hi = v.astype(BF16).astype(F32)
        return hi, v - hi

    previous_slot = None
    for r in range(ROUNDS):
        slot = plan_ref[r]
        if r == 0:
            fetch[1].wait()
            moves_inc = slot == 0
            inc = [x_ref.at[:, pl.ds(half * c, half)] for c in range(2)]
            stay = x_ref.at[:, pl.ds(b, b)]
        else:
            moves_inc = slot == previous_slot
            inc = [inc_buf.at[r - 1, c] for c in range(2)]
            stay = stay_buf.at[r - 1]
        previous_slot = slot
        sign = jnp.where(slot == 0, 1.0, -1.0).astype(F32)

        stay_f32 = stay[...].astype(F32)
        stay_sq = jnp.sum(stay_f32 * stay_f32, axis=0, keepdims=True)
        stay_hi, stay_lo = split(stay_sq)
        gram_copies = []
        for c in range(2):
            if r > 0:
                for i in range(PIECES):
                    incoming[c, i].wait_recv()
            if r == 0 and c == 0:
                fetch[0].wait()
            inc_f32 = inc[c][...].astype(F32)
            inc_hi, inc_lo = split(jnp.sum(inc_f32 * inc_f32, axis=0, keepdims=True))
            mine = gram_buf.at[r, c, d]
            mine[0:half, :] = mm_tn(inc[c][...], stay[...]).astype(BF16)
            extra = jnp.where(extra_row == 0, jnp.concatenate([inc_hi, inc_lo], axis=1), 0.0)
            extra = jnp.where(extra_row == 1, stay_hi, extra)
            extra = jnp.where(extra_row == 2, stay_lo, extra)
            mine[half:half + 16, :] = extra.astype(BF16)
            if r == 0 and c == 0:
                pl.semaphore_wait(barrier, n_pairs - 1 + n_dates - 1)
            for k in (2, 1, 3):
                copy = send(mine, mine, gram_send.at[r, c, k - 1], gram_recv.at[r, c, k - 1], (p, lax.rem(d + k, n_dates)))
                copy.start()
                gram_copies.append(copy)
        cross = []
        for c in range(2):
            for k in range(n_dates - 1):
                gram_copies[c * (n_dates - 1) + k].wait_recv()
            total = gram_buf[r, c, 0].astype(F32)
            for k in range(1, n_dates):
                total = total + gram_buf[r, c, k].astype(F32)
            inc_scale = lax.rsqrt(total[half:half + 1, :half] + total[half:half + 1, half:] + epsilon)
            stay_scale = lax.rsqrt(total[half + 1:half + 2] + total[half + 2:half + 3] + epsilon)
            inc_scale = jnp.sum(jnp.where(eye_half, inc_scale, 0.0), axis=1, keepdims=True)
            cross.append(total[0:half] * inc_scale * stay_scale)
        cross = jnp.concatenate(cross, axis=0)
        coupling = jnp.sum(jnp.sum(cross * cross, axis=0, keepdims=True), axis=1, keepdims=True)

        mine = jnp.broadcast_to(coupling * (1.0 / (b * b)), (8, 128))
        share[r] = mine
        shares[r, pl.ds(p, 1), :] = mine[0:1]
        share_copies = []
        for partner in partners:
            copy = send(share.at[r, pl.ds(0, 1)], shares.at[r, pl.ds(p, 1)], share_send.at[r], share_recv.at[r], partner)
            copy.start()
            share_copies.append(copy)

        cross_t = cross.T
        d_mov = lax.select(moves_inc, cross, cross_t)
        d_mov_t = lax.select(moves_inc, cross_t, cross)
        mov_side = Side(mm(d_mov, d_mov_t))
        stay_side = Side(mm(d_mov_t, d_mov))
        for c in range(2):
            one, two = inc[c][...], stay[:, half * c:half * (c + 1)]
            pan[:, half * c:half * (c + 1)] = lax.select(moves_inc, one, two)
            pan[:, b + half * c:b + half * (c + 1)] = lax.select(moves_inc, two, one)

        everyone = send(shares.at[r, pl.ds(0, n_pairs - 1)], shares.at[r, pl.ds(0, n_pairs - 1)], share_send.at[r],
                        share_recv.at[r], (following, d))
        everyone.wait_recv()
        overall = jnp.sum(shares[r], axis=0, keepdims=True)
        dis_ref[r:r + 1, :] = overall
        overall = overall[:, 0:1]
        damping = damping_base / jnp.sqrt(1.0 + float(b * b) * overall / n_pairs)
        n = 1.0 / (1.0 + 2.0 * damping * damping * coupling)
        t = n * damping * damping
        a = jnp.sqrt(n)
        ad = a * damping * sign

        mov_side.finish(n, t)
        top = a * mov_side.h * eye + a * mov_side.hn
        bottom = ad * mov_side.right_of(d_mov_t)
        rotation = jnp.concatenate([top, bottom], axis=0).astype(BF16)

        landing = inc_buf.at[r]
        incoming, by_relay, forwards = {}, {}, {}
        for q, (c, i) in enumerate(pieces):
            place = pl.ds(height * i, height)
            incoming[c, i] = send(mov_buf.at[r, c, place], landing.at[c, place], ring_send.at[r, q], ring_recv.at[r, q], (following, d))
            if WAYS[c][i] is None:
                continue
            way = relay_buf.at[r, q]
            by_relay[c, i] = send(mov_buf.at[r, c, place], way, relay_send.at[r, q], relay_recv.at[r, q], (relay_at[WAYS[c][i]], d))
            forwards[c, i] = send(way, landing.at[c, place], fwd_send.at[r, q], ring_recv.at[r, q], (relay_to[WAYS[c][i]], d))

        def pass_on(c, i, incoming=incoming, by_relay=by_relay):
            if WAYS[c][i] is None:
                incoming[c, i].start()
            else:
                @pl.when(is_corner)
                def _():
                    by_relay[c, i].start()

                @pl.when(jnp.logical_not(is_corner))
                def _():
                    incoming[c, i].start()

        def forward(by_relay=by_relay, forwards=forwards):
            for way, here in enumerate(is_relay):
                @pl.when(here)
                def _():
                    for c, i in pieces:
                        if WAYS[c][i] == way:
                            by_relay[c, i].wait_recv()
                            forwards[c, i].start()

        for i in range(PIECES):
            place = pl.ds(height * i, height)
            part = jnp.dot(pan[place, :], rotation, preferred_element_type=F32).astype(BF16)
            mov_buf[r, 0, place, :] = part[:, :half]
            mov_buf[r, 1, place, :] = part[:, half:]
            pass_on(0, i)
        for i in range(PIECES):
            pass_on(1, i)

        stay_side.finish(n, t)
        top = (-ad) * stay_side.right_of(d_mov)
        bottom = a * stay_side.h * eye + a * stay_side.hn
        rotation = jnp.concatenate([top, bottom], axis=0).astype(BF16)
        stay_buf[r] = jnp.dot(pan[...], rotation, preferred_element_type=F32).astype(BF16)
        forward()

        for copy in gram_copies:
            copy.wait_send()
        everyone.wait_send()
        if r == ROUNDS - 1:
            for c in range(2):
                for i in range(PIECES):
                    incoming[c, i].wait_recv()
                left, right = pl.ds(half * c, half), pl.ds(b + half * c, half)
                one, two = inc_buf[r, c], stay_buf[r, :, half * c:half * (c + 1)]
                out_ref[:, left] = lax.select(slot == 0, one, two)
                out_ref[:, right] = lax.select(slot == 0, two, one)
        def finish(incoming=incoming, by_relay=by_relay, forwards=forwards):
            for c, i in pieces:
                if WAYS[c][i] is None:
                    incoming[c, i].wait_send()
                else:
                    @pl.when(is_corner)
                    def _():
                        by_relay[c, i].wait_send()

                    @pl.when(jnp.logical_not(is_corner))
                    def _():
                        incoming[c, i].wait_send()

                    @pl.when(is_relay[WAYS[c][i]])
                    def _():
                        forwards[c, i].wait_send()
        finishes = [finish] if r == 0 else finishes + [finish]
    for finish in finishes:
        finish()


def local(n_pairs, n_dates, returns, plan):
    rows, b2 = returns.shape
    b = b2 // 2
    half = b // 2
    height = rows // PIECES
    dma = pltpu.SemaphoreType.DMA
    vmem = pl.BlockSpec(memory_space=pltpu.VMEM)
    rotated_panel, disorder = pl.pallas_call(
        functools.partial(kernel, n_pairs, n_dates),
        out_shape=(
            jax.ShapeDtypeStruct((rows, b2), BF16),
            jax.ShapeDtypeStruct((8, 128), F32),
        ),
        in_specs=[pl.BlockSpec(memory_space=pltpu.HBM), pl.BlockSpec(memory_space=pltpu.SMEM)],
        out_specs=(vmem, vmem),
        scratch_shapes=[
            pltpu.VMEM((rows, b2), BF16),
            dma((2,)),
            pltpu.VMEM((ROUNDS, 2, rows, half), BF16),
            pltpu.VMEM((ROUNDS, 2, rows, half), BF16),
            pltpu.VMEM((ROUNDS, 2 * PIECES, height, half), BF16),
            pltpu.VMEM((ROUNDS, rows, b), BF16),
            pltpu.VMEM((rows, b2), BF16),
            pltpu.VMEM((ROUNDS, 2, n_dates, half + 16, b), BF16),
            pltpu.VMEM((ROUNDS, 8, 128), F32),
            pltpu.VMEM((ROUNDS, n_pairs, 128), F32),
            dma((ROUNDS, 2 * PIECES)),
            dma((ROUNDS, 2 * PIECES)),
            dma((ROUNDS, 2 * PIECES)),
            dma((ROUNDS, 2 * PIECES)),
            dma((ROUNDS, 2 * PIECES)),
            dma((ROUNDS, 2, n_dates - 1)),
            dma((ROUNDS, 2, n_dates - 1)),
            dma((ROUNDS,)),
            dma((ROUNDS,)),
        ],
        compiler_params=pltpu.CompilerParams(collective_id=0, has_side_effects=True, vmem_limit_bytes=52 << 20),
        name="jacobi_rounds",
    )(returns, plan.reshape(ROUNDS))
    return rotated_panel, disorder[:ROUNDS, 0]


def solution(mesh):
    return jax.shard_map(
        functools.partial(local, mesh.shape["pairs"], mesh.shape["dates"]),
        mesh=mesh,
        in_specs=(P("dates", "pairs"), P(None, "pairs")),
        out_specs=(P("dates", "pairs"), P()),
        check_vma=False,
    )
```

```python
import functools

import jax
import jax.numpy as jnp
from jax import lax
from jax.experimental import pallas as pl
from jax.experimental.pallas import tpu as pltpu
from jax.sharding import PartitionSpec as P

ROUNDS = 3
damping_base = 0.5
epsilon = 1e-06
MESH = pl.DeviceIdType.MESH
F32 = jnp.float32
BF16 = jnp.bfloat16
PIECES = 8
STRAIGHT = None
WAYS = (
    (2, 0, 1, 2, 0, 1, STRAIGHT, STRAIGHT),
    (2, 0, 1, STRAIGHT, STRAIGHT, STRAIGHT, STRAIGHT, STRAIGHT),
)


def mm(a, b):
    return jnp.dot(a.astype(BF16), b.astype(BF16), preferred_element_type=F32)


def mm_tn(a, b):
    return lax.dot_general(a, b, (((0,), (0,)), ((), ())), preferred_element_type=F32)


def send(src, dst, send_sem, recv_sem, device):
    return pltpu.make_async_remote_copy(
        src_ref=src, dst_ref=dst, send_sem=send_sem, recv_sem=recv_sem, device_id=device, device_id_type=MESH
    )


def chip_steps(n_pairs):
    depth = n_pairs // 16
    places = [(dz, dy, dx) for dz in range(depth) for dy in range(4) for dx in range(4) if (dz, dy, dx) != (0, 0, 0)]

    def chips(place):
        dz, dy, dx = place
        along_z = 2 * min(dz, depth - dz) - (2 * dz == depth)
        return along_z + min(dy, 4 - dy) + min(dx, 4 - dx)

    return sorted(places, key=chips, reverse=True)


class Side:
    def __init__(self, m):
        self.m = m
        self.m2 = mm(m, m)
        self.m3 = mm(self.m2, m)

    def finish(self, n, t):
        w = 1.5 - 0.5 * n
        tau = n * w * w
        e = t * (w * w - n * w) * self.m + t * t * (0.25 * n - w) * self.m2 + (0.25 * t * t * t) * self.m3
        w1 = 1.5 - 0.5 * tau
        e2 = mm(e, e)
        y = t * self.m
        self.gb = (-0.5 * w) * e - (0.5 * w1) * y + 0.25 * mm(y, e)
        self.hb = w * w1
        e3 = mm(e, e2)
        self.f = -0.5 * ((w1 * w1 - tau * w1) * e + (0.25 * tau - w1) * e2 + 0.25 * e3)
        self.w2 = 1.5 - 0.5 * tau * w1 * w1
        self.h = self.hb * self.w2
        self.hn = self.hb * self.f + self.w2 * self.gb + mm(self.gb, self.f)

    def right_of(self, d):
        r = self.hb * d + mm(d, self.gb)
        return self.w2 * r + mm(r, self.f)


def kernel(n_pairs, n_dates, panel_ref, plan_ref, out_ref, dis_ref,
           x_ref, x_sem, inc_buf, mov_buf, relay_buf, stay_buf, pan, gram_buf, share, shares,
           ring_send, ring_recv, relay_send, relay_recv, fwd_send, gram_send, gram_recv, share_send, share_recv):
    rows, b2 = panel_ref.shape
    b = b2 // 2
    half = b // 2
    height = rows // PIECES
    plane = n_pairs // 4
    p, d = lax.axis_index("pairs"), lax.axis_index("dates")
    fetch = [pltpu.make_async_copy(panel_ref.at[:, pl.ds(b * k, b)], x_ref.at[:, pl.ds(b * k, b)], x_sem.at[k]) for k in range(2)]
    for copy in reversed(fetch):
        copy.start()
    following = lax.rem(p + 1, n_pairs)

    depth = n_pairs // 16
    pz, py, px = p // 16, lax.rem(p // 4, 4), lax.rem(p, 4)
    partners = []
    for dz, dy, dx in chip_steps(n_pairs):
        pair = lax.rem(pz + dz, depth) * 16 + lax.rem(py + dy, 4) * 4 + lax.rem(px + dx, 4)
        partners.append((pair, lax.rem(d + n_dates // 2, n_dates) if 2 * dz == depth else d))

    barrier = pltpu.get_barrier_semaphore()
    for partner in partners:
        pl.semaphore_signal(barrier, inc=1, device_id=partner, device_id_type=MESH)
    for k in range(1, n_dates):
        pl.semaphore_signal(barrier, inc=1, device_id=(p, lax.rem(d + k, n_dates)), device_id_type=MESH)

    back = (plane - 1, 3, plane - 4)
    is_corner = lax.rem(p, plane) == plane - 1
    is_relay = [lax.rem(p + k, plane) == plane - 1 for k in back]
    relay_at = [lax.rem(p - k + n_pairs, n_pairs) for k in back]
    relay_to = [lax.rem(p + k + 1, n_pairs) for k in back]

    eye_half = lax.broadcasted_iota(jnp.int32, (half, half), 0) == lax.broadcasted_iota(jnp.int32, (half, half), 1)
    eye = (lax.broadcasted_iota(jnp.int32, (b, b), 0) == lax.broadcasted_iota(jnp.int32, (b, b), 1)).astype(F32)
    extra_row = lax.broadcasted_iota(jnp.int32, (16, b), 0)
    pieces = [(c, i) for c in range(2) for i in range(PIECES)]

    def split(v):
        hi = v.astype(BF16).astype(F32)
        return hi, v - hi

    previous_slot = None
    for r in range(ROUNDS):
        slot = plan_ref[r]
        if r == 0:
            fetch[1].wait()
            moves_inc = slot == 0
            inc = [x_ref.at[:, pl.ds(half * c, half)] for c in range(2)]
            stay = x_ref.at[:, pl.ds(b, b)]
        else:
            moves_inc = slot == previous_slot
            inc = [inc_buf.at[r - 1, c] for c in range(2)]
            stay = stay_buf.at[r - 1]
        previous_slot = slot
        sign = jnp.where(slot == 0, 1.0, -1.0).astype(F32)

        stay_f32 = stay[...].astype(F32)
        stay_sq = jnp.sum(stay_f32 * stay_f32, axis=0, keepdims=True)
        stay_hi, stay_lo = split(stay_sq)
        gram_copies = []
        for c in range(2):
            if r > 0:
                for i in range(PIECES):
                    incoming[c, i].wait_recv()
            if r == 0 and c == 0:
                fetch[0].wait()
            inc_f32 = inc[c][...].astype(F32)
            inc_hi, inc_lo = split(jnp.sum(inc_f32 * inc_f32, axis=0, keepdims=True))
            mine = gram_buf.at[r, c, d]
            mine[0:half, :] = mm_tn(inc[c][...], stay[...]).astype(BF16)
            extra = jnp.where(extra_row == 0, jnp.concatenate([inc_hi, inc_lo], axis=1), 0.0)
            extra = jnp.where(extra_row == 1, stay_hi, extra)
            extra = jnp.where(extra_row == 2, stay_lo, extra)
            mine[half:half + 16, :] = extra.astype(BF16)
            if r == 0 and c == 0:
                pl.semaphore_wait(barrier, n_pairs - 1 + n_dates - 1)
            for k in (2, 3, 1):
                copy = send(mine, mine, gram_send.at[r, c, k - 1], gram_recv.at[r, c, k - 1], (p, jnp.bitwise_xor(d, k)))
                copy.start()
                gram_copies.append(copy)
        cross = []
        for c in range(2):
            for k in range(n_dates - 1):
                gram_copies[c * (n_dates - 1) + k].wait_recv()
            total = gram_buf[r, c, 0].astype(F32)
            for k in range(1, n_dates):
                total = total + gram_buf[r, c, k].astype(F32)
            inc_scale = lax.rsqrt(total[half:half + 1, :half] + total[half:half + 1, half:] + epsilon)
            stay_scale = lax.rsqrt(total[half + 1:half + 2] + total[half + 2:half + 3] + epsilon)
            inc_scale = jnp.sum(jnp.where(eye_half, inc_scale, 0.0), axis=1, keepdims=True)
            cross.append(total[0:half] * inc_scale * stay_scale)
        cross = jnp.concatenate(cross, axis=0)
        coupling = jnp.sum(jnp.sum(cross * cross, axis=0, keepdims=True), axis=1, keepdims=True)

        mine = jnp.broadcast_to(coupling * (1.0 / (b * b)), (8, 128))
        share[r] = mine
        shares[r, pl.ds(p, 1), :] = mine[0:1]
        share_copies = []
        for partner in partners:
            copy = send(share.at[r, pl.ds(0, 1)], shares.at[r, pl.ds(p, 1)], share_send.at[r], share_recv.at[r], partner)
            copy.start()
            share_copies.append(copy)

        cross_t = cross.T
        d_mov = lax.select(moves_inc, cross, cross_t)
        d_mov_t = lax.select(moves_inc, cross_t, cross)
        mov_side = Side(mm(d_mov, d_mov_t))
        stay_side = Side(mm(d_mov_t, d_mov))
        for c in range(2):
            one, two = inc[c][...], stay[:, half * c:half * (c + 1)]
            pan[:, half * c:half * (c + 1)] = lax.select(moves_inc, one, two)
            pan[:, b + half * c:b + half * (c + 1)] = lax.select(moves_inc, two, one)

        everyone = send(shares.at[r, pl.ds(0, n_pairs - 1)], shares.at[r, pl.ds(0, n_pairs - 1)], share_send.at[r],
                        share_recv.at[r], (following, d))
        everyone.wait_recv()
        overall = jnp.sum(shares[r], axis=0, keepdims=True)
        dis_ref[r:r + 1, :] = overall
        overall = overall[:, 0:1]
        damping = damping_base / jnp.sqrt(1.0 + float(b * b) * overall / n_pairs)
        n = 1.0 / (1.0 + 2.0 * damping * damping * coupling)
        t = n * damping * damping
        a = jnp.sqrt(n)
        ad = a * damping * sign

        mov_side.finish(n, t)
        top = a * mov_side.h * eye + a * mov_side.hn
        bottom = ad * mov_side.right_of(d_mov_t)
        rotation = jnp.concatenate([top, bottom], axis=0).astype(BF16)

        landing = inc_buf.at[r]
        incoming, by_relay, forwards = {}, {}, {}
        for q, (c, i) in enumerate(pieces):
            place = pl.ds(height * i, height)
            incoming[c, i] = send(mov_buf.at[r, c, place], landing.at[c, place], ring_send.at[r, q], ring_recv.at[r, q], (following, d))
            if WAYS[c][i] is None:
                continue
            way = relay_buf.at[r, q]
            by_relay[c, i] = send(mov_buf.at[r, c, place], way, relay_send.at[r, q], relay_recv.at[r, q], (relay_at[WAYS[c][i]], d))
            forwards[c, i] = send(way, landing.at[c, place], fwd_send.at[r, q], ring_recv.at[r, q], (relay_to[WAYS[c][i]], d))

        def pass_on(c, i, incoming=incoming, by_relay=by_relay):
            if WAYS[c][i] is None:
                incoming[c, i].start()
            else:
                @pl.when(is_corner)
                def _():
                    by_relay[c, i].start()

                @pl.when(jnp.logical_not(is_corner))
                def _():
                    incoming[c, i].start()

        def forward(by_relay=by_relay, forwards=forwards):
            for way, here in enumerate(is_relay):
                @pl.when(here)
                def _():
                    for c, i in pieces:
                        if WAYS[c][i] == way:
                            by_relay[c, i].wait_recv()
                            forwards[c, i].start()

        for i in range(PIECES):
            place = pl.ds(height * i, height)
            part = jnp.dot(pan[place, :], rotation, preferred_element_type=F32).astype(BF16)
            mov_buf[r, 0, place, :] = part[:, :half]
            mov_buf[r, 1, place, :] = part[:, half:]
            pass_on(0, i)
        for i in range(PIECES):
            pass_on(1, i)

        stay_side.finish(n, t)
        top = (-ad) * stay_side.right_of(d_mov)
        bottom = a * stay_side.h * eye + a * stay_side.hn
        rotation = jnp.concatenate([top, bottom], axis=0).astype(BF16)
        stay_buf[r] = jnp.dot(pan[...], rotation, preferred_element_type=F32).astype(BF16)
        forward()

        for copy in gram_copies:
            copy.wait_send()
        everyone.wait_send()
        if r == ROUNDS - 1:
            for c in range(2):
                for i in range(PIECES):
                    incoming[c, i].wait_recv()
                left, right = pl.ds(half * c, half), pl.ds(b + half * c, half)
                one, two = inc_buf[r, c], stay_buf[r, :, half * c:half * (c + 1)]
                out_ref[:, left] = lax.select(slot == 0, one, two)
                out_ref[:, right] = lax.select(slot == 0, two, one)
        def finish(incoming=incoming, by_relay=by_relay, forwards=forwards):
            for c, i in pieces:
                if WAYS[c][i] is None:
                    incoming[c, i].wait_send()
                else:
                    @pl.when(is_corner)
                    def _():
                        by_relay[c, i].wait_send()

                    @pl.when(jnp.logical_not(is_corner))
                    def _():
                        incoming[c, i].wait_send()

                    @pl.when(is_relay[WAYS[c][i]])
                    def _():
                        forwards[c, i].wait_send()
        finishes = [finish] if r == 0 else finishes + [finish]
    for finish in finishes:
        finish()


def local(n_pairs, n_dates, returns, plan):
    rows, b2 = returns.shape
    b = b2 // 2
    half = b // 2
    height = rows // PIECES
    dma = pltpu.SemaphoreType.DMA
    vmem = pl.BlockSpec(memory_space=pltpu.VMEM)
    rotated_panel, disorder = pl.pallas_call(
        functools.partial(kernel, n_pairs, n_dates),
        out_shape=(
            jax.ShapeDtypeStruct((rows, b2), BF16),
            jax.ShapeDtypeStruct((8, 128), F32),
        ),
        in_specs=[pl.BlockSpec(memory_space=pltpu.HBM), pl.BlockSpec(memory_space=pltpu.SMEM)],
        out_specs=(vmem, vmem),
        scratch_shapes=[
            pltpu.VMEM((rows, b2), BF16),
            dma((2,)),
            pltpu.VMEM((ROUNDS, 2, rows, half), BF16),
            pltpu.VMEM((ROUNDS, 2, rows, half), BF16),
            pltpu.VMEM((ROUNDS, 2 * PIECES, height, half), BF16),
            pltpu.VMEM((ROUNDS, rows, b), BF16),
            pltpu.VMEM((rows, b2), BF16),
            pltpu.VMEM((ROUNDS, 2, n_dates, half + 16, b), BF16),
            pltpu.VMEM((ROUNDS, 8, 128), F32),
            pltpu.VMEM((ROUNDS, n_pairs, 128), F32),
            dma((ROUNDS, 2 * PIECES)),
            dma((ROUNDS, 2 * PIECES)),
            dma((ROUNDS, 2 * PIECES)),
            dma((ROUNDS, 2 * PIECES)),
            dma((ROUNDS, 2 * PIECES)),
            dma((ROUNDS, 2, n_dates - 1)),
            dma((ROUNDS, 2, n_dates - 1)),
            dma((ROUNDS,)),
            dma((ROUNDS,)),
        ],
        compiler_params=pltpu.CompilerParams(collective_id=0, has_side_effects=True, vmem_limit_bytes=52 << 20),
        name="jacobi_rounds",
    )(returns, plan.reshape(ROUNDS))
    return rotated_panel, disorder[:ROUNDS, 0]


def solution(mesh):
    return jax.shard_map(
        functools.partial(local, mesh.shape["pairs"], mesh.shape["dates"]),
        mesh=mesh,
        in_specs=(P("dates", "pairs"), P(None, "pairs")),
        out_specs=(P("dates", "pairs"), P()),
        check_vma=False,
    )
```

```python
import functools

import jax
import jax.numpy as jnp
from jax import lax
from jax.experimental import pallas as pl
from jax.experimental.pallas import tpu as pltpu
from jax.sharding import PartitionSpec as P

ROUNDS = 3
damping_base = 0.5
epsilon = 1e-06
MESH = pl.DeviceIdType.MESH
F32 = jnp.float32
BF16 = jnp.bfloat16
PIECES = 8
STRAIGHT = None
WAYS = (
    (2, 0, 1, 2, 0, 1, STRAIGHT, STRAIGHT),
    (2, 0, 1, STRAIGHT, STRAIGHT, STRAIGHT, STRAIGHT, STRAIGHT),
)


def mm(a, b):
    return jnp.dot(a.astype(BF16), b.astype(BF16), preferred_element_type=F32)


def mm_tn(a, b):
    return lax.dot_general(a, b, (((0,), (0,)), ((), ())), preferred_element_type=F32)


def send(src, dst, send_sem, recv_sem, device):
    return pltpu.make_async_remote_copy(
        src_ref=src, dst_ref=dst, send_sem=send_sem, recv_sem=recv_sem, device_id=device, device_id_type=MESH
    )


def chip_steps(n_pairs):
    depth = n_pairs // 16
    places = [(dz, dy, dx) for dz in range(depth) for dy in range(4) for dx in range(4) if (dz, dy, dx) != (0, 0, 0)]

    def chips(place):
        dz, dy, dx = place
        along_z = 2 * min(dz, depth - dz) - (2 * dz == depth)
        return along_z + min(dy, 4 - dy) + min(dx, 4 - dx)

    return sorted(places, key=chips, reverse=True)


class Side:
    def __init__(self, m):
        self.m = m
        self.m2 = mm(m, m)
        self.m3 = mm(self.m2, m)

    def finish(self, n, t):
        w = 1.5 - 0.5 * n
        tau = n * w * w
        e = t * (w * w - n * w) * self.m + t * t * (0.25 * n - w) * self.m2 + (0.25 * t * t * t) * self.m3
        w1 = 1.5 - 0.5 * tau
        e2 = mm(e, e)
        y = t * self.m
        self.gb = (-0.5 * w) * e - (0.5 * w1) * y + 0.25 * mm(y, e)
        self.hb = w * w1
        e3 = mm(e, e2)
        self.f = -0.5 * ((w1 * w1 - tau * w1) * e + (0.25 * tau - w1) * e2 + 0.25 * e3)
        self.w2 = 1.5 - 0.5 * tau * w1 * w1
        self.h = self.hb * self.w2
        self.hn = self.hb * self.f + self.w2 * self.gb + mm(self.gb, self.f)

    def right_of(self, d):
        r = self.hb * d + mm(d, self.gb)
        return self.w2 * r + mm(r, self.f)


def kernel(n_pairs, n_dates, panel_ref, plan_ref, out_ref, dis_ref,
           x_ref, x_sem, inc_buf, mov_buf, relay_buf, stay_buf, pan, gram_buf, share, shares,
           ring_send, ring_recv, relay_send, relay_recv, fwd_send, gram_send, gram_recv, share_send, share_recv):
    rows, b2 = panel_ref.shape
    b = b2 // 2
    half = b // 2
    height = rows // PIECES
    plane = n_pairs // 4
    p, d = lax.axis_index("pairs"), lax.axis_index("dates")
    fetch = [pltpu.make_async_copy(panel_ref.at[:, pl.ds(b * k, b)], x_ref.at[:, pl.ds(b * k, b)], x_sem.at[k]) for k in range(2)]
    for copy in reversed(fetch):
        copy.start()
    following = lax.rem(p + 1, n_pairs)

    depth = n_pairs // 16
    pz, py, px = p // 16, lax.rem(p // 4, 4), lax.rem(p, 4)
    partners = []
    for dz, dy, dx in chip_steps(n_pairs):
        pair = lax.rem(pz + dz, depth) * 16 + lax.rem(py + dy, 4) * 4 + lax.rem(px + dx, 4)
        partners.append((pair, lax.rem(d + n_dates // 2, n_dates) if 2 * dz == depth else d))

    barrier = pltpu.get_barrier_semaphore()
    for partner in partners:
        pl.semaphore_signal(barrier, inc=1, device_id=partner, device_id_type=MESH)
    for k in range(1, n_dates):
        pl.semaphore_signal(barrier, inc=1, device_id=(p, lax.rem(d + k, n_dates)), device_id_type=MESH)

    back = (plane - 1, 3, plane - 4)
    is_corner = lax.rem(p, plane) == plane - 1
    is_relay = [lax.rem(p + k, plane) == plane - 1 for k in back]
    relay_at = [lax.rem(p - k + n_pairs, n_pairs) for k in back]
    relay_to = [lax.rem(p + k + 1, n_pairs) for k in back]

    eye_half = lax.broadcasted_iota(jnp.int32, (half, half), 0) == lax.broadcasted_iota(jnp.int32, (half, half), 1)
    eye = (lax.broadcasted_iota(jnp.int32, (b, b), 0) == lax.broadcasted_iota(jnp.int32, (b, b), 1)).astype(F32)
    extra_row = lax.broadcasted_iota(jnp.int32, (16, b), 0)
    pieces = [(c, i) for c in range(2) for i in range(PIECES)]

    def split(v):
        hi = v.astype(BF16).astype(F32)
        return hi, v - hi

    previous_slot = None
    for r in range(ROUNDS):
        slot = plan_ref[r]
        if r == 0:
            fetch[1].wait()
            moves_inc = slot == 0
            inc = [x_ref.at[:, pl.ds(half * c, half)] for c in range(2)]
            stay = x_ref.at[:, pl.ds(b, b)]
        else:
            moves_inc = slot == previous_slot
            inc = [inc_buf.at[r - 1, c] for c in range(2)]
            stay = stay_buf.at[r - 1]
        previous_slot = slot
        sign = jnp.where(slot == 0, 1.0, -1.0).astype(F32)

        stay_f32 = stay[...].astype(F32)
        stay_sq = jnp.sum(stay_f32 * stay_f32, axis=0, keepdims=True)
        stay_hi, stay_lo = split(stay_sq)
        gram_copies, arrivals = [], ([], [])
        for c in range(2):
            if r > 0:
                for i in range(PIECES):
                    incoming[c, i].wait_recv()
            if r == 0 and c == 0:
                fetch[0].wait()
            inc_f32 = inc[c][...].astype(F32)
            inc_hi, inc_lo = split(jnp.sum(inc_f32 * inc_f32, axis=0, keepdims=True))
            mine = gram_buf.at[r, c, d]
            mine[0:half, :] = mm_tn(inc[c][...], stay[...]).astype(BF16)
            extra = jnp.where(extra_row == 0, jnp.concatenate([inc_hi, inc_lo], axis=1), 0.0)
            extra = jnp.where(extra_row == 1, stay_hi, extra)
            extra = jnp.where(extra_row == 2, stay_lo, extra)
            mine[half:half + 16, :] = extra.astype(BF16)
            if r == 0 and c == 0:
                pl.semaphore_wait(barrier, n_pairs - 1 + n_dates - 1)
            for k in (2, 1) if r == 0 else (2, 3, 1):
                copy = send(mine, mine, gram_send.at[r, c, k - 1], gram_recv.at[r, c, k - 1], (p, jnp.bitwise_xor(d, k)))
                copy.start()
                gram_copies.append(copy)
                arrivals[c].append(copy)
        if r == 0:
            for c in range(2):
                arrivals[c].pop(0).wait_recv()
                other = gram_buf.at[r, c, jnp.bitwise_xor(d, 2)]
                copy = send(other, other, gram_send.at[r, c, 2], gram_recv.at[r, c, 2], (p, jnp.bitwise_xor(d, 1)))
                copy.start()
                gram_copies.append(copy)
                arrivals[c].append(copy)
        cross = []
        for c in range(2):
            for copy in arrivals[c]:
                copy.wait_recv()
            total = gram_buf[r, c, 0].astype(F32)
            for k in range(1, n_dates):
                total = total + gram_buf[r, c, k].astype(F32)
            inc_scale = lax.rsqrt(total[half:half + 1, :half] + total[half:half + 1, half:] + epsilon)
            stay_scale = lax.rsqrt(total[half + 1:half + 2] + total[half + 2:half + 3] + epsilon)
            inc_scale = jnp.sum(jnp.where(eye_half, inc_scale, 0.0), axis=1, keepdims=True)
            cross.append(total[0:half] * inc_scale * stay_scale)
        cross = jnp.concatenate(cross, axis=0)
        coupling = jnp.sum(jnp.sum(cross * cross, axis=0, keepdims=True), axis=1, keepdims=True)

        mine = jnp.broadcast_to(coupling * (1.0 / (b * b)), (8, 128))
        share[r] = mine
        shares[r, pl.ds(p, 1), :] = mine[0:1]
        share_copies = []
        for partner in partners:
            copy = send(share.at[r, pl.ds(0, 1)], shares.at[r, pl.ds(p, 1)], share_send.at[r], share_recv.at[r], partner)
            copy.start()
            share_copies.append(copy)

        cross_t = cross.T
        d_mov = lax.select(moves_inc, cross, cross_t)
        d_mov_t = lax.select(moves_inc, cross_t, cross)
        mov_side = Side(mm(d_mov, d_mov_t))
        stay_side = Side(mm(d_mov_t, d_mov))
        for c in range(2):
            one, two = inc[c][...], stay[:, half * c:half * (c + 1)]
            pan[:, half * c:half * (c + 1)] = lax.select(moves_inc, one, two)
            pan[:, b + half * c:b + half * (c + 1)] = lax.select(moves_inc, two, one)

        everyone = send(shares.at[r, pl.ds(0, n_pairs - 1)], shares.at[r, pl.ds(0, n_pairs - 1)], share_send.at[r],
                        share_recv.at[r], (following, d))
        everyone.wait_recv()
        overall = jnp.sum(shares[r], axis=0, keepdims=True)
        dis_ref[r:r + 1, :] = overall
        overall = overall[:, 0:1]
        damping = damping_base / jnp.sqrt(1.0 + float(b * b) * overall / n_pairs)
        n = 1.0 / (1.0 + 2.0 * damping * damping * coupling)
        t = n * damping * damping
        a = jnp.sqrt(n)
        ad = a * damping * sign

        mov_side.finish(n, t)
        top = a * mov_side.h * eye + a * mov_side.hn
        bottom = ad * mov_side.right_of(d_mov_t)
        rotation = jnp.concatenate([top, bottom], axis=0).astype(BF16)

        landing = inc_buf.at[r]
        incoming, by_relay, forwards = {}, {}, {}
        for q, (c, i) in enumerate(pieces):
            place = pl.ds(height * i, height)
            incoming[c, i] = send(mov_buf.at[r, c, place], landing.at[c, place], ring_send.at[r, q], ring_recv.at[r, q], (following, d))
            if WAYS[c][i] is None:
                continue
            way = relay_buf.at[r, q]
            by_relay[c, i] = send(mov_buf.at[r, c, place], way, relay_send.at[r, q], relay_recv.at[r, q], (relay_at[WAYS[c][i]], d))
            forwards[c, i] = send(way, landing.at[c, place], fwd_send.at[r, q], ring_recv.at[r, q], (relay_to[WAYS[c][i]], d))

        def pass_on(c, i, incoming=incoming, by_relay=by_relay):
            if WAYS[c][i] is None:
                incoming[c, i].start()
            else:
                @pl.when(is_corner)
                def _():
                    by_relay[c, i].start()

                @pl.when(jnp.logical_not(is_corner))
                def _():
                    incoming[c, i].start()

        def forward(by_relay=by_relay, forwards=forwards):
            for way, here in enumerate(is_relay):
                @pl.when(here)
                def _():
                    for c, i in pieces:
                        if WAYS[c][i] == way:
                            by_relay[c, i].wait_recv()
                            forwards[c, i].start()

        for i in range(PIECES):
            place = pl.ds(height * i, height)
            part = jnp.dot(pan[place, :], rotation, preferred_element_type=F32).astype(BF16)
            mov_buf[r, 0, place, :] = part[:, :half]
            mov_buf[r, 1, place, :] = part[:, half:]
            pass_on(0, i)
        for i in range(PIECES):
            pass_on(1, i)

        stay_side.finish(n, t)
        top = (-ad) * stay_side.right_of(d_mov)
        bottom = a * stay_side.h * eye + a * stay_side.hn
        rotation = jnp.concatenate([top, bottom], axis=0).astype(BF16)
        stay_buf[r] = jnp.dot(pan[...], rotation, preferred_element_type=F32).astype(BF16)
        forward()

        for copy in gram_copies:
            copy.wait_send()
        everyone.wait_send()
        if r == ROUNDS - 1:
            for c in range(2):
                for i in range(PIECES):
                    incoming[c, i].wait_recv()
                left, right = pl.ds(half * c, half), pl.ds(b + half * c, half)
                one, two = inc_buf[r, c], stay_buf[r, :, half * c:half * (c + 1)]
                out_ref[:, left] = lax.select(slot == 0, one, two)
                out_ref[:, right] = lax.select(slot == 0, two, one)
        def finish(incoming=incoming, by_relay=by_relay, forwards=forwards):
            for c, i in pieces:
                if WAYS[c][i] is None:
                    incoming[c, i].wait_send()
                else:
                    @pl.when(is_corner)
                    def _():
                        by_relay[c, i].wait_send()

                    @pl.when(jnp.logical_not(is_corner))
                    def _():
                        incoming[c, i].wait_send()

                    @pl.when(is_relay[WAYS[c][i]])
                    def _():
                        forwards[c, i].wait_send()
        finishes = [finish] if r == 0 else finishes + [finish]
    for finish in finishes:
        finish()


def local(n_pairs, n_dates, returns, plan):
    rows, b2 = returns.shape
    b = b2 // 2
    half = b // 2
    height = rows // PIECES
    dma = pltpu.SemaphoreType.DMA
    vmem = pl.BlockSpec(memory_space=pltpu.VMEM)
    rotated_panel, disorder = pl.pallas_call(
        functools.partial(kernel, n_pairs, n_dates),
        out_shape=(
            jax.ShapeDtypeStruct((rows, b2), BF16),
            jax.ShapeDtypeStruct((8, 128), F32),
        ),
        in_specs=[pl.BlockSpec(memory_space=pltpu.HBM), pl.BlockSpec(memory_space=pltpu.SMEM)],
        out_specs=(vmem, vmem),
        scratch_shapes=[
            pltpu.VMEM((rows, b2), BF16),
            dma((2,)),
            pltpu.VMEM((ROUNDS, 2, rows, half), BF16),
            pltpu.VMEM((ROUNDS, 2, rows, half), BF16),
            pltpu.VMEM((ROUNDS, 2 * PIECES, height, half), BF16),
            pltpu.VMEM((ROUNDS, rows, b), BF16),
            pltpu.VMEM((rows, b2), BF16),
            pltpu.VMEM((ROUNDS, 2, n_dates, half + 16, b), BF16),
            pltpu.VMEM((ROUNDS, 8, 128), F32),
            pltpu.VMEM((ROUNDS, n_pairs, 128), F32),
            dma((ROUNDS, 2 * PIECES)),
            dma((ROUNDS, 2 * PIECES)),
            dma((ROUNDS, 2 * PIECES)),
            dma((ROUNDS, 2 * PIECES)),
            dma((ROUNDS, 2 * PIECES)),
            dma((ROUNDS, 2, n_dates - 1)),
            dma((ROUNDS, 2, n_dates - 1)),
            dma((ROUNDS,)),
            dma((ROUNDS,)),
        ],
        compiler_params=pltpu.CompilerParams(collective_id=0, has_side_effects=True, vmem_limit_bytes=52 << 20),
        name="jacobi_rounds",
    )(returns, plan.reshape(ROUNDS))
    return rotated_panel, disorder[:ROUNDS, 0]


def solution(mesh):
    return jax.shard_map(
        functools.partial(local, mesh.shape["pairs"], mesh.shape["dates"]),
        mesh=mesh,
        in_specs=(P("dates", "pairs"), P(None, "pairs")),
        out_specs=(P("dates", "pairs"), P()),
        check_vma=False,
    )
```
